32 devices in a mesh: row: 4 (over y, x), col: 8 (over z, core).
Axes of the slice: x: 2, y: 2, z: 4, core: 2. Of those that a mesh axis runs over, the one named last changes fastest.
Arguments:
- doubles: float32 [32, 32, 192, 192], P(None, None, 'row', 'col'), may hold values from -6 to 6
- cycle_inter: float32 [6144, 6144], P('row', 'col'), may hold values from -0.078125 to 0.078125
Outputs:
- cycle_term: float32 [6144, 6144], P('row', 'col')
The draws below stay inside these ranges and needn't reach their ends.
All inputs are finite; a program needn't handle non-finite values.
Results may differ from the reference program's by a relative error of at most 0.00007.
Values sent between devices are 32-bit elements; how exact they have to be, the bound alone decides.
No kernel may reach another device: no remote copies, remote signals or barrier semaphores. Data moves between devices by JAX's collectives and lax.ppermute only.
A program may use at most 192 MiB of HBM per device.

```python
import jax
import jax.numpy as jnp
from jax import lax

O = 32
V = 192
OV = 6144


def block_levels(stream_key, extent, split, smallest, top_value):
    def one(dim, parts):
        draws = jax.random.uniform(jax.random.fold_in(jax.random.fold_in(stream_key, 6), dim), (parts,), jnp.float32, smallest / len(split), top_value / len(split))
        return jnp.repeat(jnp.exp(draws), extent[dim] // parts).reshape((-1,) + (1,) * (len(extent) - dim - 1))

    loudness = one(*split[0])
    for cut in split[1:]:
        loudness = loudness * one(*cut)
    return loudness


def noise(own_key, shape, scale, reach, split=(), held_as=jnp.bfloat16):
    drawn = jax.random.normal(own_key, shape, jnp.float32) * scale
    if len(split) > 0:
        drawn = block_levels(own_key, shape, split, -0.22, 0.18) * drawn
    return jnp.clip(drawn, min=-reach, max=reach).astype(held_as)


def setup_inputs(seed: int = 0) -> dict:
    streams_of = jax.random.split(jax.random.key(seed), 3)
    return {
        "doubles": noise(streams_of[0], (O, O, V, V), 1.0, 6.0, ((2, 4), (3, 8)), jnp.float32),
        "cycle_inter": noise(streams_of[1], (OV, OV), OV ** -0.5, 0.078125, ((0, 4), (1, 8)), jnp.float32),
    }


def reference(doubles, cycle_inter):
    amp_matrix = jnp.transpose(doubles, (0, 2, 1, 3)).reshape(O * V, O * V)
    return jnp.dot(cycle_inter, amp_matrix, precision=lax.Precision.HIGHEST, preferred_element_type=jnp.float32)
```

```python
import functools

import jax
import jax.numpy as jnp
from jax import lax
from jax.experimental import pallas as pl
from jax.experimental.pallas import tpu as pltpu
from jax.sharding import PartitionSpec as P


NT = (((1,), (1,)), ((), ()))


def params(mib):
    return pltpu.CompilerParams(vmem_limit_bytes=mib * 2**20)


def cost(flops, moved):
    return pl.CostEstimate(flops=flops, bytes_accessed=moved, transcendentals=0)


def after(x, *deps):
    return lax.optimization_barrier((x,) + deps)[0]


def pack(blocks, t, planes, received=None):
    k, j, vb, vr = t.shape
    jl = j // (2 * planes)
    rows, lanes = jl * vb, k * vr

    def fill(t_ref, put):
        for jj in range(jl):
            put(
                slice(jj * vb, (jj + 1) * vb),
                jnp.concatenate([t_ref[kk, jj] for kk in range(k)], axis=-1),
            )

    def give(blocks_ref, t_ref, o_ref):
        def put(at, x):
            o_ref[0, at] = x

        fill(t_ref, put)

    def merge(blocks_ref, t_ref, got_ref, *outs):
        for d in range(planes):

            @pl.when(pl.program_id(0) == d)
            def _():
                def put(at, x):
                    outs[d][0, at] = x

                fill(t_ref, put)
                outs[d][1] = got_ref[0]

    t_spec = pl.BlockSpec((k, jl, vb, vr), lambda i, b: (0, b[i], 0, 0))
    given = pl.BlockSpec((1, rows, lanes), lambda i, b: (i, 0, 0))
    if received is None:
        kernel, args, ins, outs = give, (), [t_spec], given
        shape = jax.ShapeDtypeStruct((planes, rows, lanes), t.dtype)
    else:
        kernel, args, ins = merge, (received,), [t_spec, given]
        outs = [pl.BlockSpec((2, rows, lanes), lambda i, b: (0, 0, 0))] * planes
        shape = [jax.ShapeDtypeStruct((2, rows, lanes), t.dtype)] * planes
    return pl.pallas_call(
        kernel,
        grid_spec=pltpu.PrefetchScalarGridSpec(
            num_scalar_prefetch=1, grid=(planes,), in_specs=ins, out_specs=outs
        ),
        out_shape=shape,
        compiler_params=params(40),
        cost_estimate=cost(0, 5 * t.size),
    )(blocks, t, *args)


def panel(where, came, planes, vb, kp, vr):
    rows_r = len(came)
    rows, lanes = came[0][0][0].shape[1:]
    jl = rows // vb
    lw = kp * vr
    vcol = 2 * planes * vb
    arrays = [x for e in came for d in e for x in d]
    index = []
    for e in range(rows_r):
        for d in range(planes):
            index += [
                (e, d, n, first)
                for n, x in enumerate(arrays)
                if any(x is y for y in came[e][d])
                for first in range(x.shape[0])
            ]

    def kernel(w_ref, *refs):
        hi_ref, lo_ref, x_ref = refs[len(arrays) :]
        p, core, r = w_ref[0], w_ref[1], w_ref[2]
        seen = {}
        for e, d, n, first in index:
            c = seen.get((e, d), 0)
            seen[e, d] = c + 1
            src = (p ^ d) * 2 + (core ^ c)
            to = pl.multiple_of(src * vb, vb)
            x_ref[r ^ e, pl.ds(to, vb)] = refs[n][first]
        for k in range(0, kp, 2):
            x = jnp.concatenate(
                [
                    x_ref[q, :, (k + kk) * vr : (k + kk + 1) * vr]
                    for kk in range(2)
                    for q in range(rows_r)
                ],
                axis=-1,
            )
            at = slice(k * rows_r * vr, (k + 2) * rows_r * vr)
            hi = x.astype(jnp.bfloat16)
            hi_ref[:, at] = hi
            lo_ref[:, at] = (x - hi.astype(jnp.float32)).astype(jnp.bfloat16)

    out = pl.BlockSpec((vcol, rows_r * lw), lambda t, j, w: (j, t))
    shape = jax.ShapeDtypeStruct((jl * vcol, rows_r * lanes), jnp.bfloat16)
    return pl.pallas_call(
        kernel,
        grid_spec=pltpu.PrefetchScalarGridSpec(
            num_scalar_prefetch=1,
            grid=(lanes // lw, jl),
            in_specs=[
                pl.BlockSpec((x.shape[0], vb, lw), lambda t, j, w: (0, j, t))
                for x in arrays
            ],
            out_specs=[out, out],
            scratch_shapes=[pltpu.VMEM((rows_r, vcol, lw), jnp.float32)],
        ),
        out_shape=[shape, shape],
        compiler_params=params(40),
        cost_estimate=cost(0, 8 * jl * vcol * rows_r * lanes),
    )(where, *arrays)


def product(a, hilo, into, start, rows):
    hi, lo = hilo
    n, depth = hi.shape
    m = a.shape[0]
    tk = depth // 8

    def kernel(a_ref, h_ref, l_ref, *refs):
        o_ref, x_ref = refs[-2:]

        @pl.when(pl.program_id(0) == 0)
        def _():
            o_ref[...] = jnp.zeros_like(o_ref)

        dot = functools.partial(
            lax.dot_general, dimension_numbers=NT, preferred_element_type=jnp.float32
        )
        x = a_ref[...]
        xh = x.astype(jnp.bfloat16)
        x_ref[:m] = xh
        x_ref[m:] = (x - xh.astype(jnp.float32)).astype(jnp.bfloat16)
        both = dot(x_ref[...], h_ref[...])
        o_ref[...] += both[:m] + both[m:] + dot(x_ref[:m], l_ref[...])

    specs = [pl.BlockSpec((m, tk), lambda i: (0, i))]
    specs += [pl.BlockSpec((n, tk), lambda i: (0, i))] * 2
    args, alias = [a, hi, lo], {}
    if into is not None:
        args.append(into)
        specs.append(pl.BlockSpec(memory_space=pl.ANY))
        alias = {3: 0}
    return pl.pallas_call(
        kernel,
        grid=(depth // tk,),
        in_specs=specs,
        out_specs=pl.BlockSpec((m, n), lambda i: (start // m, 0)),
        out_shape=jax.ShapeDtypeStruct((rows, n), jnp.float32),
        scratch_shapes=[pltpu.VMEM((2 * m, tk), jnp.bfloat16)],
        input_output_aliases=alias,
        compiler_params=params(52),
        cost_estimate=cost(6 * m * n * depth, 4 * m * depth + 4 * n * depth),
    )(*args)


def plain(doubles, cycle_inter):
    vs = doubles.shape[2] * lax.axis_size("row")
    moved = lax.all_to_all(
        lax.all_to_all(doubles, "row", split_axis=0, concat_axis=2, tiled=True),
        "col",
        split_axis=1,
        concat_axis=3,
        tiled=True,
    )
    local_panel = jnp.transpose(moved, (0, 2, 1, 3)).reshape(moved.shape[0] * vs, -1)
    amp_panel = lax.all_gather(local_panel, "row", axis=0, tiled=True)
    return jnp.dot(
        lax.all_gather(cycle_inter, "col", axis=1, tiled=True),
        amp_panel,
        precision=lax.Precision.HIGHEST,
        preferred_element_type=jnp.float32,
    )


def line(doubles, cycle_inter, rows_r, planes):
    k, j, vr, vb = doubles.shape
    col, r = lax.axis_index("col"), lax.axis_index("row")
    p, core = col // 2, col % 2
    where = jnp.stack([p, core, r]).astype(jnp.int32)

    rows = cycle_inter.shape[0]
    eighth = rows // 8
    sizes = [2 * eighth, 2 * eighth, 2 * eighth, eighth, eighth]
    starts = [sum(sizes[:i]) for i in range(len(sizes))]
    gathered = [
        lax.all_gather(cycle_inter[a : a + n], "col", axis=1, tiled=True)
        for a, n in zip(starts, sizes)
    ]

    t = jnp.transpose(doubles, (0, 1, 3, 2))
    to = 2 * (p ^ jnp.arange(planes, dtype=jnp.int32))
    give = pack((to + 1 - core).astype(jnp.int32), t, planes)
    got = lax.ppermute(give, "col", [(c, c ^ 1) for c in range(2 * planes)])
    packed = pack((to + core).astype(jnp.int32), t, planes, got)

    def across(x, bit):
        return lax.ppermute(x, "row", [(a, a ^ bit) for a in range(rows_r)])

    came = [[], [], [], []]
    for d in range(planes):
        x = packed[d]
        if d:
            pairs = [(2 * (q ^ d) + c, 2 * q + c) for q in range(planes) for c in range(2)]
            x = lax.ppermute(x, "col", pairs)
        one, two = across(x, 1), across(x, 2)
        came[0].append([x])
        came[1].append([one])
        came[2].append([two])
        came[3].append([across(one[:1], 2), across(two[1:], 1)])
    hilo = panel(where, came, planes, vb, k // planes, vr)

    result = None
    for a, start in zip(gathered, starts):
        result = product(a, hilo, result, start, rows)
    return result


def solution(mesh):
    rows_r, planes = mesh.shape["row"], mesh.shape["col"] // 2

    def body(doubles, cycle_inter):
        if rows_r == 2 * 2 and planes & (planes - 1) == 0:
            return line(doubles, cycle_inter, rows_r, planes)
        return plain(doubles, cycle_inter)

    placed = (P(None, None, "row", "col"), P("row", "col"))
    return jax.shard_map(
        body, mesh=mesh, in_specs=placed, out_specs=P("row", "col"), check_vma=False
    )
```

```python
import functools

import jax
import jax.numpy as jnp
from jax import lax
from jax.experimental import pallas as pl
from jax.experimental.pallas import tpu as pltpu
from jax.sharding import PartitionSpec as P


NT = (((1,), (1,)), ((), ()))
SIZES = (2, 2, 2, 2)


def params(mib):
    return pltpu.CompilerParams(vmem_limit_bytes=mib * 2**20)


def cost(flops, moved):
    return pl.CostEstimate(flops=flops // 4096, bytes_accessed=moved // 4096, transcendentals=0)


def after(x, *deps):
    return lax.optimization_barrier((x,) + deps)[0]


def pack(steps, t, planes, classes, received=None):
    k, j, vb, vr = t.shape
    kp = k // planes
    jl = j // (2 * planes)
    rows, lanes = jl * vb, k // 2 * vr
    kl = kp // 2
    ks = [
        [q * kp + of * kl + i for of in range(2) for q in c for i in range(kl)]
        for c in classes
    ]

    def fill(s_ref, t_ref, put):
        step = pl.program_id(0)
        for c in range(2):

            @pl.when(s_ref[2 * planes + step] == c)
            def _():
                for jj in range(jl):
                    put(
                        jj * vb,
                        jnp.concatenate([t_ref[kk, jj] for kk in ks[c]], axis=-1),
                    )

    def give(s_ref, t_ref, o_ref):
        def put(at, x):
            o_ref[0, at : at + vb] = x

        fill(s_ref, t_ref, put)

    def merge(s_ref, t_ref, got_ref, *outs):
        step = pl.program_id(0)
        first = pl.multiple_of(step % 2 * rows, rows)
        for d in range(planes):

            @pl.when(step // 2 == d)
            def _():
                def put(at, x):
                    outs[d][0, pl.ds(first + at, vb)] = x

                fill(s_ref, t_ref, put)
                outs[d][1, pl.ds(first, rows)] = got_ref[0]

    t_spec = pl.BlockSpec((k, jl, vb, vr), lambda i, b: (0, b[i], 0, 0))
    given = pl.BlockSpec((1, rows, lanes), lambda i, b: (i // 2, i % 2, 0))
    if received is None:
        kernel, args, ins, outs = give, (), [t_spec], given
        shape = jax.ShapeDtypeStruct((planes, 2 * rows, lanes), t.dtype)
    else:
        kernel, args, ins = merge, (received,), [t_spec, given]
        outs = [pl.BlockSpec((2, 2 * rows, lanes), lambda i, b: (0, 0, 0))] * planes
        shape = [jax.ShapeDtypeStruct((2, 2 * rows, lanes), t.dtype)] * planes
    return pl.pallas_call(
        kernel,
        grid_spec=pltpu.PrefetchScalarGridSpec(
            num_scalar_prefetch=1, grid=(2 * planes,), in_specs=ins, out_specs=outs
        ),
        out_shape=shape,
        compiler_params=params(40),
        cost_estimate=cost(0, 5 * t.size),
    )(steps, t, *args)


def panel(where, d, came, into, planes, vb, kp, vr):
    rows_r = len(came)
    rows, lanes = came[0][0][0].shape[1:]
    nj = rows // vb
    lw = kp * vr
    pieces = [x for e in came for x in e]
    arrays = [x for x, _, _ in pieces]
    index = []
    for n, (e, count) in enumerate((e, x[2]) for e in range(rows_r) for x in came[e]):
        index += [(e, n, i) for i in range(count)]

    def kernel(w_ref, *refs):
        hi_ref, lo_ref, x_ref = refs[-3:]
        core, r = w_ref[1], w_ref[2]
        for i, (e, n, first) in enumerate(index):
            to = pl.multiple_of((core ^ (i % 2)) * vb, vb)
            x_ref[r ^ e, pl.ds(to, vb)] = refs[n][first]
        for k in range(0, kp, 2):
            x = jnp.concatenate(
                [
                    x_ref[q, :, (k + kk) * vr : (k + kk + 1) * vr]
                    for kk in range(2)
                    for q in range(rows_r)
                ],
                axis=-1,
            )
            at = slice(k * rows_r * vr, (k + 2) * rows_r * vr)
            hi = x.astype(jnp.bfloat16)
            hi_ref[:, at] = hi
            lo_ref[:, at] = (x - hi.astype(jnp.float32)).astype(jnp.bfloat16)

    out = pl.BlockSpec((2 * vb, rows_r * lw), lambda t, j, w: (j * planes + (w[0] ^ d), t))
    shape = jax.ShapeDtypeStruct((nj * planes * 2 * vb, rows_r * lanes), jnp.bfloat16)

    def spec(at, count):
        return pl.BlockSpec((count, vb, lw), lambda t, j, w: (at // count, j, t))

    specs = [spec(at, count) for _, at, count in pieces]
    alias = {}
    if into is not None:
        alias = {1 + len(arrays): 0, 2 + len(arrays): 1}
        specs += [pl.BlockSpec(memory_space=pl.ANY)] * 2
        arrays = arrays + list(into)
    return pl.pallas_call(
        kernel,
        grid_spec=pltpu.PrefetchScalarGridSpec(
            num_scalar_prefetch=1,
            grid=(lanes // lw, nj),
            in_specs=specs,
            out_specs=[out, out],
            scratch_shapes=[pltpu.VMEM((rows_r, 2 * vb, lw), jnp.float32)],
        ),
        out_shape=[shape, shape],
        input_output_aliases=alias,
        compiler_params=params(40),
        cost_estimate=cost(0, 16 * nj * vb * rows_r * lanes),
    )(where, *arrays)


def product(where, m, offsets, own, other, hilo):
    hi, lo = hilo
    n, depth = hi.shape
    n //= 2
    per = len(offsets)
    tk = depth // (2 * per)
    operands = own + other

    def kernel(w_ref, *refs):
        ins, (h_ref, l_ref), outs = refs[: 2 * per], refs[2 * per : 2 * per + 2], refs[-3:-1]
        x_ref = refs[-1]
        step = pl.program_id(0)

        @pl.when(step == 0)
        def _():
            for o in outs:
                o[...] = jnp.zeros_like(o)

        for i, ref in enumerate(ins):

            @pl.when(step == i)
            def _():
                x = ref[...]
                xh = x.astype(jnp.bfloat16)
                x_ref[:m] = xh
                x_ref[m:] = (x - xh.astype(jnp.float32)).astype(jnp.bfloat16)

        dot = functools.partial(
            lax.dot_general, dimension_numbers=NT, preferred_element_type=jnp.float32
        )
        for i, o in enumerate(outs):
            at = slice(i * n, (i + 1) * n)
            both = dot(x_ref[...], h_ref[at])
            o[...] += both[:m] + both[m:] + dot(x_ref[:m], l_ref[at])

    def block(i, w):
        plane = w[0] ^ offsets[0]
        for n in range(1, per):
            plane = jnp.where(i % per == n, w[0] ^ offsets[n], plane)
        return 0, per * (w[1] ^ (i // per)) + plane // 2

    def rows(chunk):
        return pl.BlockSpec((m, tk), lambda i, w: (chunk, 0))

    out = pl.BlockSpec((m, n), lambda i, w: (0, 0))
    return pl.pallas_call(
        kernel,
        grid_spec=pltpu.PrefetchScalarGridSpec(
            num_scalar_prefetch=1,
            grid=(2 * per,),
            in_specs=[rows(c) for _, c in operands]
            + [pl.BlockSpec((2 * n, tk), block)] * 2,
            out_specs=[out, out],
            scratch_shapes=[pltpu.VMEM((2 * m, tk), jnp.bfloat16)],
        ),
        out_shape=[jax.ShapeDtypeStruct((m, n), jnp.float32)] * 2,
        compiler_params=params(52),
        cost_estimate=cost(12 * m * n * depth, 4 * m * depth + 8 * n * depth),
    )(where, *[x for x, _ in operands], hi, lo)


def finish(x, y, into, start, m, rows):
    n = x.shape[1]
    tm = m // 2

    def kernel(x_ref, y_ref, *refs):
        refs[-1][...] = x_ref[...] + y_ref[...]

    specs = [pl.BlockSpec((tm, n), lambda i: (i, 0))] * 2
    args, alias = [x, y], {}
    if into is not None:
        args.append(into)
        specs.append(pl.BlockSpec(memory_space=pl.ANY))
        alias = {2: 0}
    return pl.pallas_call(
        kernel,
        grid=(2,),
        in_specs=specs,
        out_specs=pl.BlockSpec((tm, n), lambda i: (start // tm + i, 0)),
        out_shape=jax.ShapeDtypeStruct((rows, n), jnp.float32),
        input_output_aliases=alias,
        compiler_params=params(40),
        cost_estimate=cost(m * n, 12 * m * n),
    )(*args)


def plain(doubles, cycle_inter):
    vs = doubles.shape[2] * lax.axis_size("row")
    moved = lax.all_to_all(
        lax.all_to_all(doubles, "row", split_axis=0, concat_axis=2, tiled=True),
        "col",
        split_axis=1,
        concat_axis=3,
        tiled=True,
    )
    local_panel = jnp.transpose(moved, (0, 2, 1, 3)).reshape(moved.shape[0] * vs, -1)
    amp_panel = lax.all_gather(local_panel, "row", axis=0, tiled=True)
    return jnp.dot(
        lax.all_gather(cycle_inter, "col", axis=1, tiled=True),
        amp_panel,
        precision=lax.Precision.HIGHEST,
        preferred_element_type=jnp.float32,
    )


def line(doubles, cycle_inter, rows_r, planes):
    k, j, vr, vb = doubles.shape
    col, r = lax.axis_index("col"), lax.axis_index("row")
    p, core = col // 2, col % 2
    where = jnp.stack([p, core, r]).astype(jnp.int32)
    kind = [(q ^ (2 * q // planes)) & 1 for q in range(planes)]
    classes = [[q for q in range(planes) if kind[q] == c] for c in range(2)]

    def send(x, pairs):
        pairs = [(2 * a + c, 2 * b + c) for a, b in pairs for c in range(2)]
        return lax.ppermute(x, "col", pairs)

    def swap(x):
        return lax.ppermute(x, "col", [(c, c ^ 1) for c in range(2 * planes)])

    trail = []

    def cross(x, d):
        x = after(x, *trail[-1:])
        trail.append(send(x, [(q ^ d, q) for q in range(planes)]))
        return trail[-1]

    rows = cycle_inter.shape[0]
    eighth = rows // 8
    sizes = [n * eighth for n in SIZES]
    starts = [sum(sizes[:i]) for i in range(len(sizes))]
    offsets = [d for d in range(planes) if kind[d] == 0]

    def take(start, size, *held):
        x = cycle_inter[start : start + size]
        return [cross(after(x, *held), d) for d in offsets[1:]]

    early = [take(0, eighth), take(eighth, sizes[0] - eighth)]
    gathered = [[jnp.concatenate(x) for x in zip(*early)]]

    t = jnp.transpose(doubles, (0, 1, 3, 2))
    to = (p ^ jnp.arange(planes, dtype=jnp.int32))[:, None] ^ jnp.arange(2)
    to_kind = jnp.take(jnp.array(kind), jnp.repeat(to[:, 0], 2))

    def steps(c):
        return jnp.concatenate([2 * to.reshape(-1) + c, to_kind]).astype(jnp.int32)

    give = pack(steps(1 - core), t, planes, classes)
    got = swap(give)
    packed = pack(steps(core), t, planes, classes, got)

    def across(x, bit):
        return lax.ppermute(x, "row", [(a, a ^ bit) for a in range(rows_r)])

    order = [0, 1] + list(range(planes - 1, 1, -1))
    parts = [packed[0]] + [None] * (planes - 1)
    links = [1 << i for i in range(rows_r.bit_length() - 1)]
    brought, hilos, hilo = [], [], None

    def block(n, e):
        if e == 0:
            return [(parts[n], 0, 2)]
        if e in links:
            return [(brought[n][e], 0, 2)]
        return [(brought[n + 1][link], 2 if n + 1 < planes else 0, 1) for link in links[::-1]]

    for n in range(planes + 1):
        if n < planes:
            d = order[n]
            if n == 1:
                x = after(packed[d], *early[0])
                parts[n] = send(x, [(q ^ d, q) for q in range(planes)])
            elif n:
                parts[n] = cross(packed[d], d)
            x = parts[n]
        else:
            gathered += [take(starts[1], sizes[1])]
        held = hilos[n - 3] if n > 2 else ()
        now = {}
        for i, link in enumerate(links):
            y = [x] if n < planes else []
            if n:
                y.append(brought[n - 1][links[1 - i]][1 - i : 2 - i])
            y = jnp.concatenate(y) if len(y) > 1 else y[0]
            now[link] = across(after(y, *held), link)
        brought.append(now)
        if n:
            pieces = [block(n - 1, e) for e in range(rows_r)]
            hilo = panel(
                where, order[n - 1], pieces, hilo, planes, vb, k // planes, vr
            )
            hilos.append(hilo)
    last = brought[-1].values()
    gathered += [take(starts[i], sizes[i], *last) for i in range(2, len(sizes))]

    result = None
    done, back = hilos[0][0], []
    own_other = swap(cycle_inter)
    for i, came in enumerate(gathered):
        came = [after(x, done) for x in came]
        other = [swap(x) for x in came]
        pieces = 1 if i + 1 < len(sizes) else 2
        m = sizes[i] // pieces
        for piece in range(pieces):
            start = starts[i] + piece * m
            came = [after(x, *back[: -1 - piece], done) for x in came]
            mine, theirs = product(
                where,
                m,
                offsets,
                [(cycle_inter, start // m)] + [(x, piece) for x in came],
                [(own_other, start // m)] + [(x, piece) for x in other],
                hilo,
            )
            done = mine
            back.append(send(theirs, [(q ^ 1, q) for q in range(planes)]))
            result = finish(mine, back[-1], result, start, m, rows)
    return result


def solution(mesh):
    rows_r, planes = mesh.shape["row"], mesh.shape["col"] // 2

    def body(doubles, cycle_inter):
        k, j, vr, vb = doubles.shape
        whole = vb % 8 == 0 and (2 * rows_r * vr) % 128 == 0 and (k // 2 * vr) % 128 == 0
        whole = whole and j % (2 * planes) == 0 and k // planes % 2 == 0
        if whole and planes > 1 and planes & (planes - 1) == 0 and rows_r == 2 * 2:
            return line(doubles, cycle_inter, rows_r, planes)
        return plain(doubles, cycle_inter)

    placed = (P(None, None, "row", "col"), P("row", "col"))
    return jax.shard_map(
        body, mesh=mesh, in_specs=placed, out_specs=P("row", "col"), check_vma=False
    )
```

```python
import functools

import jax
import jax.numpy as jnp
from jax import lax
from jax.experimental import pallas as pl
from jax.experimental.pallas import tpu as pltpu
from jax.sharding import PartitionSpec as P


NT = (((1,), (1,)), ((), ()))
SIZES = (2, 2, 2, 2)


def params(mib):
    return pltpu.CompilerParams(vmem_limit_bytes=mib * 2**20)


def cost(flops, moved):
    return pl.CostEstimate(flops=flops // 4096, bytes_accessed=moved // 4096, transcendentals=0)


def after(x, *deps):
    return lax.optimization_barrier((x,) + deps)[0]


def pack(steps, t, planes, classes, received=None):
    k, j, vb, vr = t.shape
    kp = k // planes
    jl = j // (2 * planes)
    rows, lanes = jl * vb, k // 2 * vr
    kl = kp // 2
    ks = [
        [q * kp + of * kl + i for of in range(2) for q in c for i in range(kl)]
        for c in classes
    ]

    def fill(s_ref, t_ref, put):
        step = pl.program_id(0)
        for c in range(2):

            @pl.when(s_ref[2 * planes + step] == c)
            def _():
                for jj in range(jl):
                    put(
                        jj * vb,
                        jnp.concatenate([t_ref[kk, jj] for kk in ks[c]], axis=-1),
                    )

    def give(s_ref, t_ref, o_ref):
        def put(at, x):
            o_ref[0, at : at + vb] = x

        fill(s_ref, t_ref, put)

    def merge(s_ref, t_ref, got_ref, *outs):
        step = pl.program_id(0)
        first = pl.multiple_of(step % 2 * rows, rows)
        for d in range(planes):

            @pl.when(step // 2 == d)
            def _():
                def put(at, x):
                    outs[d][0, pl.ds(first + at, vb)] = x

                fill(s_ref, t_ref, put)
                outs[d][1, pl.ds(first, rows)] = got_ref[0]

    t_spec = pl.BlockSpec((k, jl, vb, vr), lambda i, b: (0, b[i], 0, 0))
    given = pl.BlockSpec((1, rows, lanes), lambda i, b: (i // 2, i % 2, 0))
    if received is None:
        kernel, args, ins, outs = give, (), [t_spec], given
        shape = jax.ShapeDtypeStruct((planes, 2 * rows, lanes), t.dtype)
    else:
        kernel, args, ins = merge, (received,), [t_spec, given]
        outs = [pl.BlockSpec((2, 2 * rows, lanes), lambda i, b: (0, 0, 0))] * planes
        shape = [jax.ShapeDtypeStruct((2, 2 * rows, lanes), t.dtype)] * planes
    return pl.pallas_call(
        kernel,
        grid_spec=pltpu.PrefetchScalarGridSpec(
            num_scalar_prefetch=1, grid=(2 * planes,), in_specs=ins, out_specs=outs
        ),
        out_shape=shape,
        compiler_params=params(40),
        cost_estimate=cost(0, 5 * t.size),
    )(steps, t, *args)


def panel(where, d, came, into, planes, vb, kp, vr):
    rows_r = len(came)
    rows, lanes = came[0][0][0].shape[1:]
    nj = rows // vb
    lw = kp * vr
    pieces = [x for e in came for x in e]
    arrays = [x for x, _, _ in pieces]
    index = []
    for n, (e, count) in enumerate((e, x[2]) for e in range(rows_r) for x in came[e]):
        index += [(e, n, i) for i in range(count)]

    def kernel(w_ref, *refs):
        hi_ref, lo_ref, x_ref = refs[-3:]
        core, r = w_ref[1], w_ref[2]
        for i, (e, n, first) in enumerate(index):
            to = pl.multiple_of((core ^ (i % 2)) * vb, vb)
            x_ref[r ^ e, pl.ds(to, vb)] = refs[n][first]
        for k in range(0, kp, 2):
            x = jnp.concatenate(
                [
                    x_ref[q, :, (k + kk) * vr : (k + kk + 1) * vr]
                    for kk in range(2)
                    for q in range(rows_r)
                ],
                axis=-1,
            )
            at = slice(k * rows_r * vr, (k + 2) * rows_r * vr)
            hi = x.astype(jnp.bfloat16)
            hi_ref[:, at] = hi
            lo_ref[:, at] = (x - hi.astype(jnp.float32)).astype(jnp.bfloat16)

    out = pl.BlockSpec((2 * vb, rows_r * lw), lambda t, j, w: (j * planes + (w[0] ^ d), t))
    shape = jax.ShapeDtypeStruct((nj * planes * 2 * vb, rows_r * lanes), jnp.bfloat16)

    def spec(at, count):
        return pl.BlockSpec((count, vb, lw), lambda t, j, w: (at // count, j, t))

    specs = [spec(at, count) for _, at, count in pieces]
    alias = {}
    if into is not None:
        alias = {1 + len(arrays): 0, 2 + len(arrays): 1}
        specs += [pl.BlockSpec(memory_space=pl.ANY)] * 2
        arrays = arrays + list(into)
    return pl.pallas_call(
        kernel,
        grid_spec=pltpu.PrefetchScalarGridSpec(
            num_scalar_prefetch=1,
            grid=(lanes // lw, nj),
            in_specs=specs,
            out_specs=[out, out],
            scratch_shapes=[pltpu.VMEM((rows_r, 2 * vb, lw), jnp.float32)],
        ),
        out_shape=[shape, shape],
        input_output_aliases=alias,
        compiler_params=params(40),
        cost_estimate=cost(0, 16 * nj * vb * rows_r * lanes),
    )(where, *arrays)


def product(where, m, offsets, own, other, hilo):
    hi, lo = hilo
    n, depth = hi.shape
    n //= 2
    per = len(offsets)
    tk = depth // (2 * per)
    operands = own + other

    def kernel(w_ref, *refs):
        ins, (h_ref, l_ref), outs = refs[: 2 * per], refs[2 * per : 2 * per + 2], refs[-3:-1]
        x_ref = refs[-1]
        step = pl.program_id(0)

        @pl.when(step == 0)
        def _():
            for o in outs:
                o[...] = jnp.zeros_like(o)

        for i, ref in enumerate(ins):

            @pl.when(step == i)
            def _():
                x = ref[...]
                xh = x.astype(jnp.bfloat16)
                x_ref[:m] = xh
                x_ref[m:] = (x - xh.astype(jnp.float32)).astype(jnp.bfloat16)

        dot = functools.partial(
            lax.dot_general, dimension_numbers=NT, preferred_element_type=jnp.float32
        )
        for i, o in enumerate(outs):
            at = slice(i * n, (i + 1) * n)
            both = dot(x_ref[...], h_ref[at])
            o[...] += both[:m] + both[m:] + dot(x_ref[:m], l_ref[at])

    def block(i, w):
        plane = w[0] ^ offsets[0]
        for n in range(1, per):
            plane = jnp.where(i % per == n, w[0] ^ offsets[n], plane)
        return 0, per * (w[1] ^ (i // per)) + plane // 2

    def rows(chunk):
        return pl.BlockSpec((m, tk), lambda i, w: (chunk, 0))

    out = pl.BlockSpec((m, n), lambda i, w: (0, 0))
    return pl.pallas_call(
        kernel,
        grid_spec=pltpu.PrefetchScalarGridSpec(
            num_scalar_prefetch=1,
            grid=(2 * per,),
            in_specs=[rows(c) for _, c in operands]
            + [pl.BlockSpec((2 * n, tk), block)] * 2,
            out_specs=[out, out],
            scratch_shapes=[pltpu.VMEM((2 * m, tk), jnp.bfloat16)],
        ),
        out_shape=[jax.ShapeDtypeStruct((m, n), jnp.float32)] * 2,
        compiler_params=params(52),
        cost_estimate=cost(12 * m * n * depth, 4 * m * depth + 8 * n * depth),
    )(where, *[x for x, _ in operands], hi, lo)


def finish(x, y, into, start, m, rows):
    n = x.shape[1]
    tm = m // 2

    def kernel(x_ref, y_ref, *refs):
        refs[-1][...] = x_ref[...] + y_ref[...]

    specs = [pl.BlockSpec((tm, n), lambda i: (i, 0))] * 2
    args, alias = [x, y], {}
    if into is not None:
        args.append(into)
        specs.append(pl.BlockSpec(memory_space=pl.ANY))
        alias = {2: 0}
    return pl.pallas_call(
        kernel,
        grid=(2,),
        in_specs=specs,
        out_specs=pl.BlockSpec((tm, n), lambda i: (start // tm + i, 0)),
        out_shape=jax.ShapeDtypeStruct((rows, n), jnp.float32),
        input_output_aliases=alias,
        compiler_params=params(40),
        cost_estimate=cost(m * n, 12 * m * n),
    )(*args)


def plain(doubles, cycle_inter):
    vs = doubles.shape[2] * lax.axis_size("row")
    moved = lax.all_to_all(
        lax.all_to_all(doubles, "row", split_axis=0, concat_axis=2, tiled=True),
        "col",
        split_axis=1,
        concat_axis=3,
        tiled=True,
    )
    local_panel = jnp.transpose(moved, (0, 2, 1, 3)).reshape(moved.shape[0] * vs, -1)
    amp_panel = lax.all_gather(local_panel, "row", axis=0, tiled=True)
    return jnp.dot(
        lax.all_gather(cycle_inter, "col", axis=1, tiled=True),
        amp_panel,
        precision=lax.Precision.HIGHEST,
        preferred_element_type=jnp.float32,
    )


def line(doubles, cycle_inter, rows_r, planes):
    k, j, vr, vb = doubles.shape
    col, r = lax.axis_index("col"), lax.axis_index("row")
    p, core = col // 2, col % 2
    where = jnp.stack([p, core, r]).astype(jnp.int32)
    kind = [(q ^ (2 * q // planes)) & 1 for q in range(planes)]
    classes = [[q for q in range(planes) if kind[q] == c] for c in range(2)]

    def send(x, pairs):
        pairs = [(2 * a + c, 2 * b + c) for a, b in pairs for c in range(2)]
        return lax.ppermute(x, "col", pairs)

    def swap(x):
        return lax.ppermute(x, "col", [(c, c ^ 1) for c in range(2 * planes)])

    trail = []

    def cross(x, d):
        x = after(x, *trail[-1:])
        trail.append(send(x, [(q ^ d, q) for q in range(planes)]))
        return trail[-1]

    rows = cycle_inter.shape[0]
    eighth = rows // 8
    sizes = [n * eighth for n in SIZES]
    starts = [sum(sizes[:i]) for i in range(len(sizes))]
    offsets = [d for d in range(planes) if kind[d] == 0]

    def take(start, size, *held):
        x = cycle_inter[start : start + size]
        return [cross(after(x, *held), d) for d in offsets[1:]]

    t = jnp.transpose(doubles, (0, 1, 3, 2))
    to = (p ^ jnp.arange(planes, dtype=jnp.int32))[:, None] ^ jnp.arange(2)
    to_kind = jnp.take(jnp.array(kind), jnp.repeat(to[:, 0], 2))

    def steps(c):
        return jnp.concatenate([2 * to.reshape(-1) + c, to_kind]).astype(jnp.int32)

    give = pack(steps(1 - core), t, planes, classes)
    got = swap(give)
    packed = pack(steps(core), t, planes, classes, got)

    def across(x, bit):
        return lax.ppermute(x, "row", [(a, a ^ bit) for a in range(rows_r)])

    order = [0, planes - 1] + list(range(1, planes - 1))
    links = [1 << i for i in range(rows_r.bit_length() - 1)]
    parts, brought, hilos, hilo = [packed[0]], [], [], None
    first = {link: across(packed[0], link) for link in links}
    brought.append(first)
    firsts = {
        link: across(first[links[1 - i]][1 - i : 2 - i], link)
        for i, link in enumerate(links)
    }

    def block(n, e):
        if e == 0:
            return [(parts[n], 0, 2)]
        if e in links:
            return [(brought[n][e], 0, 2)]
        if n == 0:
            return [(firsts[link], 0, 1) for link in links[::-1]]
        return [(brought[n + 1][link], 2 if n + 1 < planes else 0, 1) for link in links[::-1]]

    def settle(n, hilo):
        pieces = [block(n, e) for e in range(rows_r)]
        return panel(where, order[n], pieces, hilo, planes, vb, k // planes, vr)

    sent, early = {}, []
    for n, d in enumerate(order[1:]):
        if d == 1:
            sent[d] = send(packed[d], [(q ^ d, q) for q in range(planes)])
        else:
            sent[d] = cross(packed[d], d)
        if d != 1:
            early.append(take(len(early) * eighth, eighth))
    gathered = [[jnp.concatenate(x) for x in zip(*early)]]
    for n in range(1, planes + 1):
        if n < planes:
            parts.append(sent[order[n]])
        held = tuple(firsts.values()) if n < 3 else hilos[n - 3]
        now = {}
        for i, link in enumerate(links):
            y = [parts[n]] if n < planes else []
            if n > 1:
                y.append(brought[n - 1][links[1 - i]][1 - i : 2 - i])
            y = jnp.concatenate(y) if len(y) > 1 else y[0]
            now[link] = across(after(y, *held), link)
        brought.append(now)
        if n == planes:
            gathered += [take(starts[1], sizes[1])]
        if n > 1:
            hilo = settle(n - 1, hilo)
        else:
            hilo = settle(0, None)
        hilos.append(hilo)
    last = brought[-1].values()
    gathered += [take(starts[i], sizes[i], *last) for i in range(2, len(sizes))]

    result = None
    done, back = hilos[0][0], []
    own_other = swap(cycle_inter)
    for i, came in enumerate(gathered):
        came = [after(x, done) for x in came]
        other = [swap(x) for x in came]
        pieces = 1 if i + 1 < len(sizes) else 2
        m = sizes[i] // pieces
        for piece in range(pieces):
            start = starts[i] + piece * m
            came = [after(x, *back[: -1 - piece], done) for x in came]
            mine, theirs = product(
                where,
                m,
                offsets,
                [(cycle_inter, start // m)] + [(x, piece) for x in came],
                [(own_other, start // m)] + [(x, piece) for x in other],
                hilo,
            )
            done = mine
            back.append(send(theirs, [(q ^ 1, q) for q in range(planes)]))
            result = finish(mine, back[-1], result, start, m, rows)
    return result


def solution(mesh):
    rows_r, planes = mesh.shape["row"], mesh.shape["col"] // 2

    def body(doubles, cycle_inter):
        k, j, vr, vb = doubles.shape
        whole = vb % 8 == 0 and (2 * rows_r * vr) % 128 == 0 and (k // 2 * vr) % 128 == 0
        whole = whole and j % (2 * planes) == 0 and k // planes % 2 == 0
        if whole and planes > 1 and planes & (planes - 1) == 0 and rows_r == 2 * 2:
            return line(doubles, cycle_inter, rows_r, planes)
        return plain(doubles, cycle_inter)

    placed = (P(None, None, "row", "col"), P("row", "col"))
    return jax.shard_map(
        body, mesh=mesh, in_specs=placed, out_specs=P("row", "col"), check_vma=False
    )
```

```python
import functools

import jax
import jax.numpy as jnp
from jax import lax
from jax.experimental import pallas as pl
from jax.experimental.pallas import tpu as pltpu
from jax.sharding import PartitionSpec as P


NT = (((1,), (1,)), ((), ()))
SIZES = (2, 2, 2, 2)


def params(mib):
    return pltpu.CompilerParams(vmem_limit_bytes=mib * 2**20)


def cost(flops, moved):
    return pl.CostEstimate(flops=flops // 4096, bytes_accessed=moved // 4096, transcendentals=0)


def after(x, *deps):
    return lax.optimization_barrier((x,) + deps)[0]


def pack(steps, t, planes, classes, received=None):
    k, j, vb, vr = t.shape
    kp = k // planes
    jl = j // (2 * planes)
    rows, lanes = jl * vb, k // 2 * vr
    kl = kp // 2
    ks = [
        [q * kp + of * kl + i for of in range(2) for q in c for i in range(kl)]
        for c in classes
    ]

    def fill(s_ref, t_ref, put):
        step = pl.program_id(0)
        for c in range(2):

            @pl.when(s_ref[2 * planes + step] == c)
            def _():
                for jj in range(jl):
                    put(
                        jj * vb,
                        jnp.concatenate([t_ref[kk, jj] for kk in ks[c]], axis=-1),
                    )

    def give(s_ref, t_ref, o_ref):
        def put(at, x):
            o_ref[0, at : at + vb] = x

        fill(s_ref, t_ref, put)

    def merge(s_ref, t_ref, got_ref, *outs):
        step = pl.program_id(0)
        first = pl.multiple_of(step % 2 * rows, rows)
        for d in range(planes):

            @pl.when(step // 2 == d)
            def _():
                def put(at, x):
                    outs[d][0, pl.ds(first + at, vb)] = x

                fill(s_ref, t_ref, put)
                outs[d][1, pl.ds(first, rows)] = got_ref[0]

    t_spec = pl.BlockSpec((k, jl, vb, vr), lambda i, b: (0, b[i], 0, 0))
    given = pl.BlockSpec((1, rows, lanes), lambda i, b: (i // 2, i % 2, 0))
    if received is None:
        kernel, args, ins, outs = give, (), [t_spec], given
        shape = jax.ShapeDtypeStruct((planes, 2 * rows, lanes), t.dtype)
    else:
        kernel, args, ins = merge, (received,), [t_spec, given]
        outs = [pl.BlockSpec((2, 2 * rows, lanes), lambda i, b: (0, 0, 0))] * planes
        shape = [jax.ShapeDtypeStruct((2, 2 * rows, lanes), t.dtype)] * planes
    return pl.pallas_call(
        kernel,
        grid_spec=pltpu.PrefetchScalarGridSpec(
            num_scalar_prefetch=1, grid=(2 * planes,), in_specs=ins, out_specs=outs
        ),
        out_shape=shape,
        compiler_params=params(40),
        cost_estimate=cost(0, 5 * t.size),
    )(steps, t, *args)


def panel(where, d, came, into, planes, vb, kp, vr):
    rows_r = len(came)
    rows, lanes = came[0][0][0].shape[1:]
    nj = rows // vb
    lw = kp * vr
    pieces = [x for e in came for x in e]
    arrays = [x for x, _, _ in pieces]
    index = []
    for n, (e, count) in enumerate((e, x[2]) for e in range(rows_r) for x in came[e]):
        index += [(e, n, i) for i in range(count)]

    def kernel(w_ref, *refs):
        hi_ref, lo_ref, x_ref = refs[-3:]
        core, r = w_ref[1], w_ref[2]
        for i, (e, n, first) in enumerate(index):
            to = pl.multiple_of((core ^ (i % 2)) * vb, vb)
            x_ref[r ^ e, pl.ds(to, vb)] = refs[n][first]
        for k in range(0, kp, 2):
            x = jnp.concatenate(
                [
                    x_ref[q, :, (k + kk) * vr : (k + kk + 1) * vr]
                    for kk in range(2)
                    for q in range(rows_r)
                ],
                axis=-1,
            )
            at = slice(k * rows_r * vr, (k + 2) * rows_r * vr)
            hi = x.astype(jnp.bfloat16)
            hi_ref[:, at] = hi
            lo_ref[:, at] = (x - hi.astype(jnp.float32)).astype(jnp.bfloat16)

    out = pl.BlockSpec((2 * vb, rows_r * lw), lambda t, j, w: (j * planes + (w[0] ^ d), t))
    shape = jax.ShapeDtypeStruct((nj * planes * 2 * vb, rows_r * lanes), jnp.bfloat16)

    def spec(at, count):
        return pl.BlockSpec((count, vb, lw), lambda t, j, w: (at // count, j, t))

    specs = [spec(at, count) for _, at, count in pieces]
    alias = {}
    if into is not None:
        alias = {1 + len(arrays): 0, 2 + len(arrays): 1}
        specs += [pl.BlockSpec(memory_space=pl.ANY)] * 2
        arrays = arrays + list(into)
    return pl.pallas_call(
        kernel,
        grid_spec=pltpu.PrefetchScalarGridSpec(
            num_scalar_prefetch=1,
            grid=(lanes // lw, nj),
            in_specs=specs,
            out_specs=[out, out],
            scratch_shapes=[pltpu.VMEM((rows_r, 2 * vb, lw), jnp.float32)],
        ),
        out_shape=[shape, shape],
        input_output_aliases=alias,
        compiler_params=params(40),
        cost_estimate=cost(0, 16 * nj * vb * rows_r * lanes),
    )(where, *arrays)


def product(where, m, offsets, own, other, hilo):
    hi, lo = hilo
    n, depth = hi.shape
    n //= 2
    per = len(offsets)
    tk = depth // (2 * per)
    pieces, places = [], []
    for i, operand in enumerate(own + other):
        at = 0
        for piece in operand:
            pieces.append(piece)
            places.append((i, at, at + piece[2]))
            at += piece[2]

    def kernel(w_ref, *refs):
        ins, (h_ref, l_ref), outs = refs[:-5], refs[-5:-3], refs[-3:-1]
        x_ref = refs[-1]
        step = pl.program_id(0)

        @pl.when(step == 0)
        def _():
            for o in outs:
                o[...] = jnp.zeros_like(o)

        for (i, at, end), ref in zip(places, ins):

            @pl.when(step == i)
            def _():
                x = ref[...]
                xh = x.astype(jnp.bfloat16)
                x_ref[at:end] = xh
                x_ref[m + at : m + end] = (x - xh.astype(jnp.float32)).astype(
                    jnp.bfloat16
                )

        dot = functools.partial(
            lax.dot_general, dimension_numbers=NT, preferred_element_type=jnp.float32
        )
        for i, o in enumerate(outs):
            at = slice(i * n, (i + 1) * n)
            both = dot(x_ref[...], h_ref[at])
            o[...] += both[:m] + both[m:] + dot(x_ref[:m], l_ref[at])

    def block(i, w):
        plane = w[0] ^ offsets[0]
        for n in range(1, per):
            plane = jnp.where(i % per == n, w[0] ^ offsets[n], plane)
        return 0, per * (w[1] ^ (i // per)) + plane // 2

    def rows(chunk, size):
        return pl.BlockSpec((size, tk), lambda i, w: (chunk, 0))

    out = pl.BlockSpec((m, n), lambda i, w: (0, 0))
    return pl.pallas_call(
        kernel,
        grid_spec=pltpu.PrefetchScalarGridSpec(
            num_scalar_prefetch=1,
            grid=(2 * per,),
            in_specs=[rows(c, size) for _, c, size in pieces]
            + [pl.BlockSpec((2 * n, tk), block)] * 2,
            out_specs=[out, out],
            scratch_shapes=[pltpu.VMEM((2 * m, tk), jnp.bfloat16)],
        ),
        out_shape=[jax.ShapeDtypeStruct((m, n), jnp.float32)] * 2,
        compiler_params=params(52),
        cost_estimate=cost(12 * m * n * depth, 4 * m * depth + 8 * n * depth),
    )(where, *[x for x, _, _ in pieces], hi, lo)


def finish(x, y, into, start, tm, rows):
    m, n = x.shape

    def kernel(x_ref, y_ref, *refs):
        refs[-1][...] = x_ref[...] + y_ref[...]

    specs = [pl.BlockSpec((tm, n), lambda i: (i, 0))] * 2
    args, alias = [x, y], {}
    if into is not None:
        args.append(into)
        specs.append(pl.BlockSpec(memory_space=pl.ANY))
        alias = {2: 0}
    return pl.pallas_call(
        kernel,
        grid=(m // tm,),
        in_specs=specs,
        out_specs=pl.BlockSpec((tm, n), lambda i: (start // tm + i, 0)),
        out_shape=jax.ShapeDtypeStruct((rows, n), jnp.float32),
        input_output_aliases=alias,
        compiler_params=params(40),
        cost_estimate=cost(m * n, 12 * m * n),
    )(*args)


def plain(doubles, cycle_inter):
    vs = doubles.shape[2] * lax.axis_size("row")
    moved = lax.all_to_all(
        lax.all_to_all(doubles, "row", split_axis=0, concat_axis=2, tiled=True),
        "col",
        split_axis=1,
        concat_axis=3,
        tiled=True,
    )
    local_panel = jnp.transpose(moved, (0, 2, 1, 3)).reshape(moved.shape[0] * vs, -1)
    amp_panel = lax.all_gather(local_panel, "row", axis=0, tiled=True)
    return jnp.dot(
        lax.all_gather(cycle_inter, "col", axis=1, tiled=True),
        amp_panel,
        precision=lax.Precision.HIGHEST,
        preferred_element_type=jnp.float32,
    )


def line(doubles, cycle_inter, rows_r, planes):
    k, j, vr, vb = doubles.shape
    col, r = lax.axis_index("col"), lax.axis_index("row")
    p, core = col // 2, col % 2
    where = jnp.stack([p, core, r]).astype(jnp.int32)
    kind = [(q ^ (2 * q // planes)) & 1 for q in range(planes)]
    classes = [[q for q in range(planes) if kind[q] == c] for c in range(2)]

    def send(x, pairs):
        pairs = [(2 * a + c, 2 * b + c) for a, b in pairs for c in range(2)]
        return lax.ppermute(x, "col", pairs)

    def swap(x):
        return lax.ppermute(x, "col", [(c, c ^ 1) for c in range(2 * planes)])

    trail = []

    def cross(x, d):
        x = after(x, *trail[-1:])
        trail.append(send(x, [(q ^ d, q) for q in range(planes)]))
        return trail[-1]

    rows = cycle_inter.shape[0]
    eighth = rows // 8
    sizes = [n * eighth for n in SIZES]
    starts = [sum(sizes[:i]) for i in range(len(sizes))]
    offsets = [d for d in range(planes) if kind[d] == 0]

    def take(start, size, *held):
        x = cycle_inter[start : start + size]
        return [cross(after(x, *held), d) for d in offsets[1:]]

    t = jnp.transpose(doubles, (0, 1, 3, 2))
    to = (p ^ jnp.arange(planes, dtype=jnp.int32))[:, None] ^ jnp.arange(2)
    to_kind = jnp.take(jnp.array(kind), jnp.repeat(to[:, 0], 2))

    def steps(c):
        return jnp.concatenate([2 * to.reshape(-1) + c, to_kind]).astype(jnp.int32)

    give = pack(steps(1 - core), t, planes, classes)
    got = swap(give)
    packed = pack(steps(core), t, planes, classes, got)

    def across(x, bit):
        return lax.ppermute(x, "row", [(a, a ^ bit) for a in range(rows_r)])

    order = [0, planes - 1] + list(range(1, planes - 1))
    links = [1 << i for i in range(rows_r.bit_length() - 1)]
    parts, brought, hilos, hilo = [packed[0]], [], [], None
    first = {link: across(packed[0], link) for link in links}
    brought.append(first)
    firsts = {
        link: across(first[links[1 - i]][1 - i : 2 - i], link)
        for i, link in enumerate(links)
    }

    def block(n, e):
        if e == 0:
            return [(parts[n], 0, 2)]
        if e in links:
            return [(brought[n][e], 0, 2)]
        if n == 0:
            return [(firsts[link], 0, 1) for link in links[::-1]]
        return [(brought[n + 1][link], 2 if n + 1 < planes else 0, 1) for link in links[::-1]]

    def settle(n, hilo):
        pieces = [block(n, e) for e in range(rows_r)]
        return panel(where, order[n], pieces, hilo, planes, vb, k // planes, vr)

    sent, early = {}, []
    for n, d in enumerate(order[1:]):
        if d == 1:
            sent[d] = send(packed[d], [(q ^ d, q) for q in range(planes)])
        else:
            sent[d] = cross(packed[d], d)
        if d != 1:
            early.append(take(len(early) * eighth, eighth))
    gathered = [[jnp.concatenate(x) for x in zip(*early)]]
    for n in range(1, planes + 1):
        if n < planes:
            parts.append(sent[order[n]])
        held = tuple(firsts.values()) if n < 3 else hilos[n - 3]
        now = {}
        for i, link in enumerate(links):
            y = [parts[n]] if n < planes else []
            if n > 1:
                y.append(brought[n - 1][links[1 - i]][1 - i : 2 - i])
            y = jnp.concatenate(y) if len(y) > 1 else y[0]
            now[link] = across(after(y, *held), link)
        brought.append(now)
        if n == planes:
            gathered += [take(starts[1], sizes[1])]
        if n > 1:
            hilo = settle(n - 1, hilo)
        else:
            hilo = settle(0, None)
        hilos.append(hilo)
    last = brought[-1].values()
    gathered += [take(starts[i], sizes[i], *last) for i in range(2, len(sizes))]

    result = None
    done, back = hilos[0][0], []
    own_other = swap(cycle_inter)
    for start, m, came in zip(starts, sizes, gathered):
        came = [after(x, done) for x in came]
        other = [swap(x) for x in came]
        came = [after(x, *back[:-1], done) for x in came]
        at = range(start // eighth, (start + m) // eighth)

        def operands(whole, parts):
            own = [(whole, n, eighth) for n in at]
            return [own] + [[(x, 0, m)] for x in parts]

        mine, theirs = product(
            where, m, offsets, operands(cycle_inter, came), operands(own_other, other), hilo
        )
        done = mine
        back.append(send(theirs, [(q ^ 1, q) for q in range(planes)]))
        result = finish(mine, back[-1], result, start, eighth, rows)
    return result


def solution(mesh):
    rows_r, planes = mesh.shape["row"], mesh.shape["col"] // 2

    def body(doubles, cycle_inter):
        k, j, vr, vb = doubles.shape
        whole = vb % 8 == 0 and (2 * rows_r * vr) % 128 == 0 and (k // 2 * vr) % 128 == 0
        whole = whole and j % (2 * planes) == 0 and k // planes % 2 == 0
        if whole and planes > 1 and planes & (planes - 1) == 0 and rows_r == 2 * 2:
            return line(doubles, cycle_inter, rows_r, planes)
        return plain(doubles, cycle_inter)

    placed = (P(None, None, "row", "col"), P("row", "col"))
    return jax.shard_map(
        body, mesh=mesh, in_specs=placed, out_specs=P("row", "col"), check_vma=False
    )
```
